512 devices in a mesh: dp: 32 (over z_lo, x, core), seq: 16 (over y, z_hi).
Axes of the slice: x: 4, y: 4, z: 16 (z_hi: 4, z_lo: 4; z = z_hi * 4 + z_lo), core: 2. Of those that a mesh axis runs over, the one named last changes fastest.
Arguments:
- normed: bfloat16 [32, 2048, 4096], P('dp', 'seq'), may hold values from -6 to 6
- frozen_query_key_value: bfloat16 [32, 2048, 16, 384], P('dp', 'seq'), may hold values from -6 to 6
- frames: int32 [32, 2048], P('dp'), may hold values from 0 to 15, as said below
- adapter_query_key_value_down: bfloat16 [4096, 64], replicated, may hold values from -0.09375 to 0.09375
- adapter_query_key_value_up: bfloat16 [64, 16, 384], P(None, 'seq'), may hold values from -0.75 to 0.75
- adapter_output_down: bfloat16 [16, 128, 64], P('seq'), may hold values from -0.125 to 0.125
- adapter_output_up: bfloat16 [64, 4096], P(None, 'seq'), may hold values from -0.75 to 0.75
- readout: bfloat16 [4096, 128], P('seq'), may hold values from -0.09375 to 0.09375
- frozen_readout_head: bfloat16 [16, 128, 128], P('seq'), may hold values from -0.125 to 0.125
- residual_velocity: bfloat16 [32, 2048, 128], P('dp'), may hold values from -6 to 6
- sampling_velocity: bfloat16 [32, 2048, 128], P('dp'), may hold values from -12 to 12
- sampler_step_noise: bfloat16 [32, 2048, 128], P('dp'), may hold values from -5 to 5
- rewards: float32 [32], replicated, may hold values from -4 to 4
- rollout_group_index: int32 [32], replicated, may hold values from 0 to 7, never falling along the last dimension, each value on 1 to 6 neighbouring positions
- denoising_step_index: int32 [1], replicated, may hold values from 1 to 3
Outputs:
- grad_in: float32 [4096, 64], P(('dp', 'seq'))
- grad_qkv: float32 [64, 16, 384], P('dp', 'seq')
- grad_out_in: float32 [16, 128, 64], P('seq', None, 'dp')
- grad_out: float32 [64, 4096], P('dp', 'seq')
The draws below stay inside these ranges and needn't reach their ends.
Inputs may be any that keep to these rules, and one draw needn't show every extreme that they name: `rollout_group_index`: rollouts of one group stand next to each other; a group holds 1 to 6 rollouts. `frames`: each rollout's tokens carry every frame number on 128 tokens, in a drawn order.
All inputs are finite; a program needn't handle non-finite values.
Results may differ from the reference program's by a relative error of at most 0.022.
Values may be sent and summed in bfloat16 or wider, within the bound.
No kernel may reach another device: no remote copies, remote signals or barrier semaphores. Data moves between devices by JAX's collectives and lax.ppermute only.
A program may use at most 64 MiB of HBM per device.

```python
import math
import jax
import jax.numpy as jnp
import numpy as np
from jax import lax

MODEL_WIDTH = 4096
LOCAL_HEADS = 16
HEAD_WIDTH = 128
ADAPTER_RANK = 64
CH = 128
FRAMES = 16
STEPS = 10
LENGTH = 2048
ROLLOUTS = 32
GROUPS = 8


def draw_frozen_query_key_value(key, part):
    key = jax.random.fold_in(key, 11)
    array_shape = (ROLLOUTS, LENGTH, LOCAL_HEADS, 3 * HEAD_WIDTH)
    first_key = jax.random.fold_in(key, 0)
    return jnp.clip(jax.random.normal(first_key, array_shape, jnp.float32), -5.0, 5.0).astype(jnp.bfloat16)


def draw_sampling_velocity(key, part):
    key = jax.random.fold_in(key, 23)
    scale_key, value_key = jax.random.split(key)
    scales = jnp.exp(jax.random.uniform(scale_key, (ROLLOUTS, 1, 1), jnp.float32, math.log(0.3), math.log(3.0)))
    values = jnp.clip(jax.random.normal(value_key, (ROLLOUTS, LENGTH, CH), jnp.float32), -4.0, 4.0)
    return (values * scales).astype(jnp.bfloat16)


def draw_frames(key, part):
    key = jax.random.fold_in(key, 37)
    labels = jnp.arange(LENGTH, dtype=jnp.int32) * FRAMES // LENGTH
    rollout_keys = jax.random.split(key, ROLLOUTS)

    def shuffle_one(single_key):
        return jax.random.permutation(single_key, labels)
    return jax.vmap(shuffle_one)(rollout_keys).astype(jnp.int32)


def shard_levels(key, dims, pieces, least, high):
    level = 1.0
    for dim, parts in pieces:
        steps = jax.random.uniform(jax.random.fold_in(jax.random.fold_in(key, 6), dim), (parts,), jnp.float32, least / len(pieces), high / len(pieces))
        level = level * jnp.repeat(jnp.exp(steps), dims[dim] // parts).reshape((-1,) + (1,) * (len(dims) - 1 - dim))
    return level


def length_profile(number_of, total, most, lean):
    weights = [(1 << 20) // math.isqrt(rank ** lean) + 1 for rank in range(2, number_of + 1)]
    rest, counts = total - most - (number_of - 1), [1] * (number_of - 1)
    while rest > 0:
        candidates = [i for i in range(number_of - 1) if counts[i] < most]
        mass, left = sum([weights[i] for i in candidates]), rest
        for i in candidates:
            addition = min(most - counts[i], max(1, left * weights[i] // mass), rest)
            counts[i] = counts[i] + addition
            rest = rest - addition
    return np.array([most] + counts)


def ragged_sizes(own_key, count, total, reach, lean):
    if count == 2:
        one = jax.random.randint(own_key, (), max(1, total - reach), min(reach, total - 1) + 1)
        return jnp.stack([one, total - one])
    lengths = jnp.asarray(length_profile(count, total, reach, lean), jnp.int32)
    pairs = (count - 1) // 2
    donor, sink = lengths[1:1 + 2 * pairs:2], lengths[2:2 + 2 * pairs:2]
    room = jnp.minimum(donor - 1, reach - sink)
    moved = jax.random.randint(jax.random.fold_in(own_key, 1), (pairs,), 0, 1 << 20) % (room + 1)
    lengths = lengths.at[1:1 + 2 * pairs:2].set(donor - moved).at[2:2 + 2 * pairs:2].set(sink + moved)
    return lengths[jax.random.permutation(jax.random.fold_in(own_key, 2), count)]


def noise(key, extent, width, limit, cuts=(), kind=jnp.bfloat16):
    array = jax.random.normal(key, extent, jnp.float32) * width
    if len(cuts) > 0:
        array = shard_levels(key, extent, cuts, -0.22, 0.18) * array
    return jnp.clip(array, min=-limit, max=limit).astype(kind)


def setup_inputs(seed: int = 0) -> dict:
    splits = jax.random.split(jax.random.key(seed), 16)
    return {
        "normed": noise(splits[0], (ROLLOUTS, LENGTH, MODEL_WIDTH), 1.0, 6.0, ((0, 32), (1, 16))),
        "frozen_query_key_value": draw_frozen_query_key_value(jax.random.fold_in(splits[15], 71), 0),
        "frames": draw_frames(jax.random.fold_in(splits[15], 71), 0),
        "adapter_query_key_value_down": noise(splits[3], (MODEL_WIDTH, ADAPTER_RANK), MODEL_WIDTH ** -0.5, 0.09375),
        "adapter_query_key_value_up": noise(splits[4], (ADAPTER_RANK, LOCAL_HEADS, 3 * HEAD_WIDTH), ADAPTER_RANK ** -0.5, 0.75, ((1, 16),)),
        "adapter_output_down": noise(splits[5], (LOCAL_HEADS, HEAD_WIDTH, ADAPTER_RANK), (LOCAL_HEADS * HEAD_WIDTH) ** -0.5, 0.125, ((0, 16),)),
        "adapter_output_up": noise(splits[6], (ADAPTER_RANK, MODEL_WIDTH), ADAPTER_RANK ** -0.5, 0.75, ((1, 16),)),
        "readout": noise(splits[7], (MODEL_WIDTH, CH), MODEL_WIDTH ** -0.5, 0.09375, ((0, 16),)),
        "frozen_readout_head": noise(splits[8], (LOCAL_HEADS, HEAD_WIDTH, CH), (LOCAL_HEADS * HEAD_WIDTH) ** -0.5, 0.125, ((0, 16),)),
        "residual_velocity": noise(splits[9], (ROLLOUTS, LENGTH, CH), 1.0, 6.0, ((0, 32),)),
        "sampling_velocity": draw_sampling_velocity(jax.random.fold_in(splits[15], 71), 0),
        "sampler_step_noise": noise(splits[11], (ROLLOUTS, LENGTH, CH), 1.0, 5.0, ((0, 32),)),
        "rewards": noise(splits[12], (ROLLOUTS,), 1.0, 4.0, (), jnp.float32),
        "rollout_group_index": jnp.searchsorted(jnp.cumsum(ragged_sizes(splits[13], GROUPS, ROLLOUTS, 6, 0)), jnp.arange(ROLLOUTS), side="right").astype(jnp.int32),
        "denoising_step_index": jax.random.randint(splits[14], (1,), 1, 4).astype(jnp.int32),
    }


ADAPTER_SCALE = 1.0
ROPE_BASE = 10000.0
ETA = 0.7
CLIP = 0.05
ADV_FLOOR = 0.5

def rope_tables(frame_row, head_size):
    half_size = head_size // 2
    inverse = ROPE_BASE ** (-jnp.arange(half_size, dtype=jnp.float32) / half_size)
    angles = frame_row.astype(jnp.float32)[:, None] * inverse[None, :]
    return (jnp.cos(angles), jnp.sin(angles))

def rotate(tensor, cosine_table, sine_table, direction):
    half_size = tensor.shape[-1] // 2
    first_half = tensor[..., :half_size]
    second_half = tensor[..., half_size:]
    cosine_rows = cosine_table[:, None, :]
    sine_rows = direction * sine_table[:, None, :]
    return jnp.concatenate([first_half * cosine_rows - second_half * sine_rows, first_half * sine_rows + second_half * cosine_rows], axis=-1)

def gap_factor(denoising_step_index, total_steps):
    noise_level = 1.0 - denoising_step_index[0].astype(jnp.float32) / total_steps
    step_width = 1.0 / total_steps
    sigma_value = ETA * jnp.sqrt(noise_level / (1.0 - noise_level))
    spread = sigma_value * math.sqrt(step_width)
    drift_coef = sigma_value * sigma_value / (2.0 * noise_level)
    return step_width * (1.0 + drift_coef * (1.0 - noise_level)) / spread

def advantages(rewards, rollout_group_index):
    same_group = (rollout_group_index[:, None] == rollout_group_index[None, :]).astype(jnp.float32)
    group_size = lax.optimization_barrier(jnp.sum(same_group, axis=1))
    group_mean = lax.optimization_barrier(jnp.sum(same_group * rewards[None, :], axis=1)) / group_size
    centred = rewards[None, :] - group_mean[:, None]
    group_var = lax.optimization_barrier(jnp.sum(same_group * centred * centred, axis=1)) / group_size
    return (rewards - group_mean) / jnp.maximum(jnp.sqrt(group_var), ADV_FLOOR)

def clip_weight(logratio, advantage):
    ratio = jnp.exp(logratio)
    active = jnp.where(advantage >= 0.0, ratio <= 1.0 + CLIP, ratio >= 1.0 - CLIP)
    return jnp.where(active, advantage * ratio, 0.0)

def head_probs(query_head, key_head):
    scores = jnp.dot(query_head, key_head.T, preferred_element_type=jnp.float32) * (1.0 / math.sqrt(HEAD_WIDTH))
    return jax.nn.softmax(scores, axis=-1).astype(jnp.bfloat16)

def head_forward(head_parts):
    query_head, key_head, value_head = head_parts
    soft_weights = head_probs(query_head, key_head)
    return jnp.dot(soft_weights, value_head, preferred_element_type=jnp.float32).astype(jnp.bfloat16)

def head_backward(head_parts):
    query_head, key_head, value_head, attn_head, grad_head = head_parts
    att_scale = 1.0 / math.sqrt(HEAD_WIDTH)
    soft_weights = head_probs(query_head, key_head)
    row_delta = lax.optimization_barrier(jnp.sum(grad_head.astype(jnp.float32) * attn_head.astype(jnp.float32), axis=1))
    prob_grad = jnp.dot(grad_head, value_head.T, preferred_element_type=jnp.float32)
    score_grad = (soft_weights.astype(jnp.float32) * (prob_grad - row_delta[:, None])).astype(jnp.bfloat16)
    query_grad = jnp.dot(score_grad, key_head, preferred_element_type=jnp.float32) * att_scale
    key_grad = jnp.dot(score_grad.T, query_head, preferred_element_type=jnp.float32) * att_scale
    value_grad = jnp.dot(soft_weights.T, grad_head, preferred_element_type=jnp.float32)
    return (query_grad, key_grad, value_grad)

def rollout_loss_terms(entries, adapter_query_key_value_down, adapter_query_key_value_up, adapter_output_down, frozen_readout_head, readout_rows, multiplier):
    normalized_rows, frozen_rows, frame_row, frozen_velocity_rows, old_vel, noise_rows, advantage = entries
    down_projected_rows = jnp.dot(normalized_rows, adapter_query_key_value_down, preferred_element_type=jnp.float32).astype(jnp.bfloat16)
    query_key_value_single = frozen_rows.astype(jnp.float32) + ADAPTER_SCALE * jnp.einsum('il,lgf->igf', down_projected_rows.astype(jnp.float32), adapter_query_key_value_up.astype(jnp.float32))
    cosine_table, sine_table = rope_tables(frame_row, HEAD_WIDTH)
    queries = rotate(query_key_value_single[..., :HEAD_WIDTH], cosine_table, sine_table, 1.0).astype(jnp.bfloat16)
    keys_all = rotate(query_key_value_single[..., HEAD_WIDTH:2 * HEAD_WIDTH], cosine_table, sine_table, 1.0).astype(jnp.bfloat16)
    values = query_key_value_single[..., 2 * HEAD_WIDTH:].astype(jnp.bfloat16)
    by_head = (jnp.swapaxes(queries, 0, 1), jnp.swapaxes(keys_all, 0, 1), jnp.swapaxes(values, 0, 1))
    attention_block = jnp.swapaxes(lax.map(head_forward, by_head), 0, 1)
    velocity_piece = jnp.einsum('thd,hdc->tc', attention_block.astype(jnp.float32), frozen_readout_head.astype(jnp.float32))
    output_down_rows = jnp.einsum('nok,okf->nf', attention_block.astype(jnp.float32), adapter_output_down.astype(jnp.float32)).astype(jnp.bfloat16)
    predicted_velocity = frozen_velocity_rows.astype(jnp.float32) + velocity_piece + ADAPTER_SCALE * jnp.dot(output_down_rows, readout_rows, preferred_element_type=jnp.float32)
    scaled_gap = multiplier * (predicted_velocity - old_vel.astype(jnp.float32))
    noise_float = noise_rows.astype(jnp.float32)
    logratio = -jnp.sum(noise_float * scaled_gap + 0.5 * scaled_gap * scaled_gap) / (LENGTH * CH)
    rollout_weight = clip_weight(logratio, advantage)
    velocity_gradient = (-(rollout_weight * multiplier) * (noise_float + scaled_gap)).astype(jnp.bfloat16)
    output_down_gradient = (ADAPTER_SCALE * jnp.dot(velocity_gradient, readout_rows.T, preferred_element_type=jnp.float32)).astype(jnp.bfloat16)
    readout_gradient = ADAPTER_SCALE * jnp.dot(output_down_rows.T, velocity_gradient, preferred_element_type=jnp.float32)
    attention_gradient = (jnp.einsum('zo,pjo->zpj', velocity_gradient.astype(jnp.float32), frozen_readout_head.astype(jnp.float32)) + jnp.einsum('js,bps->jbp', output_down_gradient.astype(jnp.float32), adapter_output_down.astype(jnp.float32))).astype(jnp.bfloat16)
    out_in_grad = jnp.einsum('thd,tr->hdr', attention_block.astype(jnp.float32), output_down_gradient.astype(jnp.float32))
    query_grad, key_grad, value_grad = lax.map(head_backward, by_head + (jnp.swapaxes(attention_block, 0, 1), jnp.swapaxes(attention_gradient, 0, 1)))
    query_grad = rotate(jnp.swapaxes(query_grad, 0, 1), cosine_table, sine_table, -1.0)
    key_grad = rotate(jnp.swapaxes(key_grad, 0, 1), cosine_table, sine_table, -1.0)
    value_grad = jnp.swapaxes(value_grad, 0, 1)
    query_key_value_row_gradient = jnp.concatenate([query_grad, key_grad, value_grad], axis=-1).astype(jnp.bfloat16)
    query_key_value_gradient = ADAPTER_SCALE * jnp.einsum('jm,jba->mba', down_projected_rows.astype(jnp.float32), query_key_value_row_gradient.astype(jnp.float32))
    down_gradient = (ADAPTER_SCALE * jnp.einsum('wiq,diq->wd', query_key_value_row_gradient.astype(jnp.float32), adapter_query_key_value_up.astype(jnp.float32))).astype(jnp.bfloat16)
    in_grad = jnp.dot(normalized_rows.T, down_gradient, preferred_element_type=jnp.float32)
    return (in_grad, query_key_value_gradient, out_in_grad, readout_gradient)

def reference(normed, frozen_query_key_value, frames, adapter_query_key_value_down, adapter_query_key_value_up, adapter_output_down, adapter_output_up, readout, frozen_readout_head, residual_velocity, sampling_velocity, sampler_step_noise, rewards, rollout_group_index, denoising_step_index):
    readout_rows = jnp.dot(adapter_output_up, readout, preferred_element_type=jnp.float32).astype(jnp.bfloat16)
    multiplier = gap_factor(denoising_step_index, STEPS)
    advantage = advantages(rewards, rollout_group_index)

    def one_rollout(entries):
        return rollout_loss_terms(entries, adapter_query_key_value_down, adapter_query_key_value_up, adapter_output_down, frozen_readout_head, readout_rows, multiplier)
    in_parts, qkv_parts, out_in_parts, fold_parts = lax.map(one_rollout, (normed, frozen_query_key_value, frames, residual_velocity, sampling_velocity, sampler_step_noise, advantage))
    fold_total = lax.optimization_barrier(jnp.sum(fold_parts, axis=0))
    grad_out = jnp.dot(fold_total, readout.astype(jnp.float32).T, precision=lax.Precision.HIGHEST)
    return (lax.optimization_barrier(jnp.sum(in_parts, axis=0)), lax.optimization_barrier(jnp.sum(qkv_parts, axis=0)), lax.optimization_barrier(jnp.sum(out_in_parts, axis=0)), grad_out)
```

```python
import functools
import math

import jax
import jax.numpy as jnp
from jax import lax
from jax.experimental import pallas as pl
from jax.experimental.pallas import tpu as pltpu
from jax.sharding import Mesh
from jax.sharding import PartitionSpec as P

STEPS = 10
ROPE_BASE = 10000.0
ETA = 0.7
CLIP = 0.05
ADV_FLOOR = 0.5

NAMES = ("zlo", "x", "core", "y", "zhi")
SIZES = (4, 4, 2, 4, 4)
DP = ("zlo", "x", "core")
SEQ = ("y", "zhi")
XC = ("x", "core")
Z = ("zlo", "zhi")

HEADS = 4
TOK = 128
OWN = 512
LENGTH = 2048
HD = 128
RANK = 64
SCALE = 1.0 / math.sqrt(HD)
F32 = jnp.float32
BF16 = jnp.bfloat16
VMEM_LIMIT = 56 * 1024 * 1024


def exchange(pieces, axes):
    return lax.all_to_all(pieces, axes, split_axis=0, concat_axis=0, tiled=True)


def spread(value, axes, count):
    return exchange(jnp.broadcast_to(value[None], (count,) + value.shape), axes)


def dot(a, b, dims=(1, 0)):
    return lax.dot_general(a, b, (((dims[0],), (dims[1],)), ((), ())), preferred_element_type=F32)


def gap_factor(denoising_step_index):
    noise_level = 1.0 - denoising_step_index[0].astype(F32) / STEPS
    step_width = 1.0 / STEPS
    sigma_value = ETA * jnp.sqrt(noise_level / (1.0 - noise_level))
    spread_value = sigma_value * math.sqrt(step_width)
    drift_coef = sigma_value * sigma_value / (2.0 * noise_level)
    return step_width * (1.0 + drift_coef * (1.0 - noise_level)) / spread_value


def advantages(rewards, rollout_group_index):
    same_group = (rollout_group_index[:, None] == rollout_group_index[None, :]).astype(F32)
    group_size = jnp.sum(same_group, axis=1)
    group_mean = jnp.sum(same_group * rewards[None, :], axis=1) / group_size
    centred = rewards[None, :] - group_mean[:, None]
    group_var = jnp.sum(same_group * centred * centred, axis=1) / group_size
    return (rewards - group_mean) / jnp.maximum(jnp.sqrt(group_var), ADV_FLOOR)


def clip_weight(logratio, advantage):
    ratio = jnp.exp(logratio)
    active = jnp.where(advantage >= 0.0, ratio <= 1.0 + CLIP, ratio >= 1.0 - CLIP)
    return jnp.where(active, advantage * ratio, 0.0)


def rope_tables(frame_row):
    half = HD // 2
    inverse = ROPE_BASE ** (-jnp.arange(half, dtype=F32) / half)
    angles = frame_row.astype(F32)[:, None] * inverse[None, :]
    cos, sin = jnp.cos(angles), jnp.sin(angles)
    return jnp.concatenate([cos, cos], axis=1), jnp.concatenate([-sin, sin], axis=1)


def swap_halves(tensor):
    half = HD // 2
    return jnp.concatenate([tensor[..., half:], tensor[..., :half]], axis=-1)


def forward_kernel(q_ref, k_ref, v_ref, rh_ref, ad_ref, folded_ref, att_ref, prob_ref, inv_ref, vel_ref, od_ref, vel_acc, od_acc):
    head = pl.program_id(0)
    scores = dot(k_ref[0], q_ref[0], (1, 1))
    peak = jnp.max(scores, axis=0, keepdims=True)
    weights = jnp.exp((scores - peak) * SCALE)
    inverse = 1.0 / jnp.sum(weights, axis=0, keepdims=True)
    weights = weights.astype(BF16)
    prob_ref[0] = weights
    inv_ref[0] = inverse
    attended = dot(v_ref[0], weights, (0, 0)) * inverse
    att = attended.T.astype(BF16)
    att_ref[0] = att
    velocity = dot(att, rh_ref[0])
    down = dot(att, ad_ref[0])

    @pl.when(head == 0)
    def _():
        vel_acc[...] = velocity
        od_acc[...] = down

    @pl.when(head > 0)
    def _():
        vel_acc[...] += velocity
        od_acc[...] += down

    @pl.when(head == HEADS - 1)
    def _():
        out_down = od_acc[...].astype(BF16)
        od_ref[...] = out_down
        vel_ref[...] = (vel_acc[...] + dot(out_down, folded_ref[...])).astype(BF16)


def forward(q, k, v, rh, ad, folded):
    per_head = lambda *dims: pl.BlockSpec((1,) + dims, lambda h: (h,) + (0,) * len(dims))
    whole = lambda *dims: pl.BlockSpec(dims, lambda h: (0,) * len(dims))
    return pl.pallas_call(
        forward_kernel,
        grid=(HEADS,),
        in_specs=[
            per_head(OWN, HD),
            per_head(LENGTH, HD),
            per_head(LENGTH, HD),
            per_head(HD, HD),
            per_head(HD, RANK),
            whole(RANK, HD),
        ],
        out_specs=[
            per_head(OWN, HD),
            per_head(LENGTH, OWN),
            per_head(1, OWN),
            whole(OWN, HD),
            whole(OWN, RANK),
        ],
        out_shape=[
            jax.ShapeDtypeStruct((HEADS, OWN, HD), BF16),
            jax.ShapeDtypeStruct((HEADS, LENGTH, OWN), BF16),
            jax.ShapeDtypeStruct((HEADS, 1, OWN), F32),
            jax.ShapeDtypeStruct((OWN, HD), BF16),
            jax.ShapeDtypeStruct((OWN, RANK), BF16),
        ],
        scratch_shapes=[pltpu.VMEM((OWN, HD), F32), pltpu.VMEM((OWN, RANK), F32)],
        compiler_params=pltpu.CompilerParams(vmem_limit_bytes=VMEM_LIMIT),
        name="attention_forward",
    )(q, k, v, rh, ad, folded)


def unrotate(grad, cos, sin):
    return (grad * cos - pltpu.roll(grad, HD // 2, 1) * sin).astype(BF16)


def backward_kernel(
    y_ref, q_ref, k_ref, v_ref, prob_ref, inv_ref, att_ref, g_ref, og_ref, rh_ref, ad_ref, up_ref,
    down_ref, own_ref, cos_ref, sin_ref, cos_own_ref, sin_own_ref, dgrad_ref, qkv_ref, oi_ref, dg_acc, own_acc,
):
    head = pl.program_id(0)
    att = att_ref[0]
    og = og_ref[...]
    att_grad = (dot(g_ref[...], rh_ref[0], (1, 1)) + dot(og, ad_ref[0], (1, 1))).astype(BF16)
    att_grad = att_grad.astype(F32)
    inverse = inv_ref[0]
    delta = jnp.sum((att_grad * att.astype(F32)).T, axis=0, keepdims=True) * inverse
    scaled = (att_grad * jnp.broadcast_to(inverse, (HD, OWN)).T).astype(BF16)
    weights = prob_ref[0]
    prob_grad = dot(v_ref[0], scaled, (1, 1))
    score_grad = (weights.astype(F32) * (prob_grad - delta)).astype(BF16)
    v_grad = dot(weights, scaled).astype(BF16)
    k_grad = unrotate(dot(score_grad, q_ref[0]) * SCALE, cos_ref[...], sin_ref[...])
    q_grad = dot(k_ref[0], score_grad, (0, 0)) * SCALE
    q_grad = unrotate(q_grad.T, cos_own_ref[...], sin_own_ref[...])
    up = up_ref[0]
    share = dot(k_grad, up[:, HD : 2 * HD], (1, 1)) + dot(v_grad, up[:, 2 * HD :], (1, 1))

    q_share = dot(q_grad, up[:, :HD], (1, 1))

    @pl.when(head == 0)
    def _():
        dg_acc[...] = share
        own_acc[...] = q_share

    @pl.when(head > 0)
    def _():
        dg_acc[...] += share
        own_acc[...] += q_share

    qkv_ref[0, :, :HD] = dot(own_ref[...], q_grad, (0, 0)).astype(BF16)
    qkv_ref[0, :, HD : 2 * HD] = dot(down_ref[...], k_grad, (0, 0)).astype(BF16)
    qkv_ref[0, :, 2 * HD :] = dot(down_ref[...], v_grad, (0, 0)).astype(BF16)
    oi_ref[0] = dot(og, att, (0, 0)).astype(BF16)

    @pl.when(head == HEADS - 1)
    def _():
        dgrad_ref[...] = dg_acc[...].astype(BF16)
        mine = pl.ds(pl.multiple_of(y_ref[0] * OWN, OWN), OWN)
        dgrad_ref[mine, :] = (dg_acc[mine, :] + own_acc[...]).astype(BF16)


def backward(y, q, k, v, prob, inv, att, g, og, rh, ad, up, down, own, cos, sin, cos_own, sin_own):
    per_head = lambda *dims: pl.BlockSpec((1,) + dims, lambda h: (h,) + (0,) * len(dims))
    whole = lambda *dims: pl.BlockSpec(dims, lambda h: (0,) * len(dims))
    return pl.pallas_call(
        backward_kernel,
        grid=(HEADS,),
        in_specs=[
            pl.BlockSpec(memory_space=pltpu.SMEM),
            per_head(OWN, HD),
            per_head(LENGTH, HD),
            per_head(LENGTH, HD),
            per_head(LENGTH, OWN),
            per_head(1, OWN),
            per_head(OWN, HD),
            whole(OWN, HD),
            whole(OWN, RANK),
            per_head(HD, HD),
            per_head(HD, RANK),
            per_head(RANK, 3 * HD),
            whole(LENGTH, RANK),
            whole(OWN, RANK),
            whole(LENGTH, HD),
            whole(LENGTH, HD),
            whole(OWN, HD),
            whole(OWN, HD),
        ],
        out_specs=[whole(LENGTH, RANK), per_head(RANK, 3 * HD), per_head(RANK, HD)],
        out_shape=[
            jax.ShapeDtypeStruct((LENGTH, RANK), BF16),
            jax.ShapeDtypeStruct((HEADS, RANK, 3 * HD), BF16),
            jax.ShapeDtypeStruct((HEADS, RANK, HD), BF16),
        ],
        scratch_shapes=[pltpu.VMEM((LENGTH, RANK), F32), pltpu.VMEM((OWN, RANK), F32)],
        compiler_params=pltpu.CompilerParams(vmem_limit_bytes=VMEM_LIMIT),
        name="attention_backward",
    )(y, q, k, v, prob, inv, att, g, og, rh, ad, up, down, own, cos, sin, cos_own, sin_own)


def fold_lanes(rows):
    n = rows.shape[0] // 2
    return jnp.concatenate([rows[:n], rows[n:]], axis=1)


def unfold_lanes(rows):
    return jnp.concatenate([rows[..., :64], rows[..., 64:]], axis=-2)


def body(
    normed,
    frozen,
    frames,
    qkv_down,
    qkv_up,
    out_down_adapter,
    out_up,
    readout,
    readout_head,
    residual_velocity,
    sampling_velocity,
    sampler_step_noise,
    rewards,
    rollout_group_index,
    denoising_step_index,
):
    y = lax.axis_index("y")
    zhi = lax.axis_index("zhi")
    multiplier = gap_factor(denoising_step_index)
    advantage = advantages(rewards, rollout_group_index)[lax.axis_index(DP)]

    pack = jnp.concatenate(
        [qkv_up[:, 0, :HD], qkv_up[:, 0, HD : 2 * HD], qkv_up[:, 0, 2 * HD :], out_down_adapter[0].T, readout_head[0]]
    )
    pack = spread(pack, "y", 4)
    up = jnp.concatenate([pack[:, :64], pack[:, 64:128], pack[:, 128:192]], axis=2)
    ad = jnp.swapaxes(pack[:, 192:256], 1, 2)
    rh = pack[:, 256:]

    down_rows = dot(normed[0], qkv_down).astype(BF16)
    fold_part = dot(out_up, readout).astype(BF16)
    parts = frozen[0].reshape(TOK, 4, 4, 3, HD).transpose(2, 3, 1, 0, 4)
    extra = jnp.concatenate([fold_lanes(down_rows), fold_part])
    extra = jnp.broadcast_to(extra[None], (4,) + extra.shape)
    send_kv = jnp.concatenate([parts[:, 1:].reshape(4, 8 * TOK, HD), extra], axis=1)
    send_q = parts[:, 0].reshape(4, 4 * TOK, HD)
    got_kv = exchange(send_kv, "zhi")
    got_q = exchange(send_q, "zhi")

    down_own = unfold_lanes(got_kv[:, 8 * TOK : 8 * TOK + 64]).reshape(OWN, RANK)
    fold_z = jnp.sum(got_kv[:, 8 * TOK + 64 :].astype(F32), axis=0).astype(BF16)
    cos, sin = rope_tables(frames[0])
    cos_own = lax.dynamic_slice_in_dim(cos, y * OWN, OWN, 0)
    sin_own = lax.dynamic_slice_in_dim(sin, y * OWN, OWN, 0)
    update = jnp.einsum("tr,hrd->htd", down_own, up, preferred_element_type=F32)

    def tokens(block):
        return block.reshape(4, 4, TOK, HD).swapaxes(0, 1).reshape(4, OWN, HD).astype(F32)

    def rotated(tensor):
        return (tensor * cos_own + swap_halves(tensor) * sin_own).astype(BF16)

    k_own = rotated(tokens(got_kv[:, : 4 * TOK]) + update[..., HD : 2 * HD])
    v_own = (tokens(got_kv[:, 4 * TOK : 8 * TOK]) + update[..., 2 * HD :]).astype(BF16)
    shared = jnp.concatenate(
        [k_own.reshape(4 * OWN, HD), v_own.reshape(4 * OWN, HD), fold_lanes(down_own), fold_z]
    )
    shared = lax.all_gather(shared, "y", axis=0, tiled=False)
    k = shared[:, : 4 * OWN].reshape(4, 4, OWN, HD).swapaxes(0, 1).reshape(4, LENGTH, HD)
    v = shared[:, 4 * OWN : 8 * OWN].reshape(4, 4, OWN, HD).swapaxes(0, 1).reshape(4, LENGTH, HD)
    down_all = unfold_lanes(shared[:, 8 * OWN : 8 * OWN + 256]).reshape(LENGTH, RANK)
    folded = jnp.sum(shared[:, 8 * OWN + 256 :].astype(F32), axis=0).astype(BF16)
    q = rotated(tokens(got_q) + update[..., :HD])

    att, prob, inv, vel_part, out_down = forward(q, k, v, rh, ad, folded)

    velocity = jnp.sum(spread(vel_part, "zhi", 4).astype(F32), axis=0)
    own = lambda array: lax.dynamic_slice_in_dim(array[0], y * OWN, OWN, 0).astype(F32)
    gap = multiplier * (own(residual_velocity) + velocity - own(sampling_velocity))
    noise = own(sampler_step_noise)
    log_part = -jnp.sum(noise * gap + 0.5 * gap * gap) / (LENGTH * HD)
    g = (noise + gap).astype(BF16)
    og = dot(g, folded, (1, 1)).astype(BF16)
    fold_grad = dot(out_down, g, (0, 0)).astype(BF16)

    down_grad, qkv_grad, oi_grad = backward(
        y[None].astype(jnp.int32), q, k, v, prob, inv, att, g, og, rh, ad, up, down_all, down_own, cos, sin, cos_own, sin_own
    )

    high = lax.reduce_precision(log_part, 8, 7)
    middle = lax.reduce_precision(log_part - high, 8, 7)
    low = lax.reduce_precision(log_part - high - middle, 8, 7)
    lane = lax.broadcasted_iota(jnp.int32, (16, HD), 1)
    log_rows = jnp.where(lane == 0, high, jnp.where(lane == 1, middle, jnp.where(lane == 2, low, 0.0)))
    send = jnp.concatenate(
        [
            jnp.stack([fold_lanes(b) for b in down_grad.reshape(4, OWN, RANK)]),
            qkv_grad[:, :, :HD],
            qkv_grad[:, :, HD : 2 * HD],
            qkv_grad[:, :, 2 * HD :],
            oi_grad,
            jnp.broadcast_to(fold_grad[None], (4, RANK, HD)),
            jnp.broadcast_to(log_rows.astype(BF16)[None], (4, 16, HD)),
        ],
        axis=1,
    )
    got = exchange(send, "y").astype(F32)
    total = jnp.sum(got, axis=0)
    logratio = jnp.sum(total[576, :3])
    weight = -(clip_weight(logratio, advantage) * multiplier)
    small = jnp.concatenate([total[256 + 64 * i : 320 + 64 * i] for i in range(5)], axis=1) * weight
    down_z = (unfold_lanes(total[:256]) * weight).astype(BF16)

    down_z = jnp.stack([fold_lanes(b) for b in down_z.reshape(4, TOK, RANK)])
    down_z = jnp.sum(exchange(down_z, "zhi").astype(F32), axis=0)
    down_z = unfold_lanes(down_z).astype(BF16)
    halves = [dot(normed[0][:, half * 2048 : half * 2048 + 2048], down_z, (0, 0)) for half in range(2)]
    in_part = jnp.concatenate(halves, axis=1).astype(BF16)
    in_part = in_part.reshape(16, 4, 32, 128).swapaxes(0, 1).reshape(4, 512, 128)
    in_part = jnp.sum(exchange(in_part, "y").astype(F32), axis=0)

    in_part = in_part.reshape(2, 8, 32, 128).swapaxes(0, 1).reshape(8, 64, 128)
    small = small.reshape(4, 8, 2, 5, HD).transpose(1, 0, 2, 3, 4).reshape(8, 40, HD)
    small = jnp.concatenate([small, jnp.zeros((8, 8, HD), F32)], axis=1)
    both = jnp.concatenate([in_part, small], axis=1).astype(BF16)
    both = jnp.sum(exchange(both, XC).astype(F32), axis=0)
    in_part = both[:64].reshape(2, 4, 8, 2, 64).transpose(3, 0, 1, 2, 4).reshape(4, 4, 4, HD)
    small = both[64:104].reshape(4, 1, 10, HD)
    here = (lax.broadcasted_iota(jnp.int32, (4, 4, 10, HD), 1) == zhi).astype(F32)
    everywhere = lax.broadcasted_iota(jnp.int32, (4, 4, 10, HD), 2) % 5 == 4
    small = small * jnp.where(everywhere, 1.0, here)
    last = jnp.concatenate([in_part, small, jnp.zeros((4, 4, 2, HD), F32)], axis=2).astype(BF16)
    last = jnp.sum(exchange(last.reshape(16, 16, HD), Z).astype(F32), axis=0)
    grad_in = last[:4].reshape(8, 64)
    small = last[4:14].reshape(2, 5, HD)
    grad_qkv = small[:, None, :3].reshape(2, 1, 3 * HD)
    grad_out_in = small[:, 3].T[None]
    grad_out = lax.dot_general(
        small[:, 4], readout.astype(F32), (((1,), (1,)), ((), ())), precision=lax.Precision.HIGHEST
    )
    return grad_in, grad_qkv, grad_out_in, grad_out


def solution(mesh):
    mesh = Mesh(mesh.devices.reshape(SIZES), NAMES)
    in_specs = (
        P(DP, SEQ, None),
        P(DP, SEQ, None, None),
        P(DP, None),
        P(),
        P(None, SEQ, None),
        P(SEQ, None, None),
        P(None, SEQ),
        P(SEQ, None),
        P(SEQ, None, None),
        P(DP, None, None),
        P(DP, None, None),
        P(DP, None, None),
        P(),
        P(),
        P(),
    )
    out_specs = (P(DP + SEQ, None), P(DP, SEQ, None), P(SEQ, None, DP), P(DP, SEQ))
    return jax.shard_map(body, mesh=mesh, in_specs=in_specs, out_specs=out_specs, check_vma=False)
```

```python
import math

import jax
import jax.numpy as jnp
from jax import lax
from jax.experimental import pallas as pl
from jax.experimental.pallas import tpu as pltpu
from jax.sharding import Mesh
from jax.sharding import PartitionSpec as P

STEPS = 10
ROPE_BASE = 10000.0
ETA = 0.7
CLIP = 0.05
ADV_FLOOR = 0.5

NAMES = ("zlo", "x", "core", "y", "zhi")
SIZES = (4, 4, 2, 4, 4)
DP = ("zlo", "x", "core")
SEQ = ("y", "zhi")
XC = ("x", "core")
Z = ("zlo", "zhi")

HEADS = 4
TOK = 128
OWN = 512
LENGTH = 2048
HD = 128
RANK = 64
SCALE = 1.0 / math.sqrt(HD)
F32 = jnp.float32
BF16 = jnp.bfloat16
VMEM_LIMIT = 56 * 1024 * 1024


def exchange(pieces, axes):
    return lax.all_to_all(pieces, axes, split_axis=0, concat_axis=0, tiled=True)


def dot(a, b, dims=(1, 0)):
    return lax.dot_general(a, b, (((dims[0],), (dims[1],)), ((), ())), preferred_element_type=F32)


def gap_factor(denoising_step_index):
    noise_level = 1.0 - denoising_step_index[0].astype(F32) / STEPS
    step_width = 1.0 / STEPS
    sigma_value = ETA * jnp.sqrt(noise_level / (1.0 - noise_level))
    spread_value = sigma_value * math.sqrt(step_width)
    drift_coef = sigma_value * sigma_value / (2.0 * noise_level)
    return step_width * (1.0 + drift_coef * (1.0 - noise_level)) / spread_value


def advantages(rewards, rollout_group_index):
    same_group = (rollout_group_index[:, None] == rollout_group_index[None, :]).astype(F32)
    group_size = jnp.sum(same_group, axis=1)
    group_mean = jnp.sum(same_group * rewards[None, :], axis=1) / group_size
    centred = rewards[None, :] - group_mean[:, None]
    group_var = jnp.sum(same_group * centred * centred, axis=1) / group_size
    return (rewards - group_mean) / jnp.maximum(jnp.sqrt(group_var), ADV_FLOOR)


def rope_tables(frame_row):
    half = HD // 2
    inverse = ROPE_BASE ** (-jnp.arange(half, dtype=F32) / half)
    angles = frame_row.astype(F32)[:, None] * inverse[None, :]
    cos, sin = jnp.cos(angles), jnp.sin(angles)
    return jnp.concatenate([cos, cos], axis=1), jnp.concatenate([-sin, sin], axis=1)


def call(kernel, name, grid, in_specs, out_specs, out_shape, scratch=(), prefetch=0):
    return pl.pallas_call(
        kernel,
        grid_spec=pltpu.PrefetchScalarGridSpec(
            num_scalar_prefetch=prefetch,
            grid=grid,
            in_specs=in_specs,
            out_specs=out_specs,
            scratch_shapes=list(scratch),
        ),
        out_shape=out_shape,
        compiler_params=pltpu.CompilerParams(vmem_limit_bytes=VMEM_LIMIT),
        name=name,
    )


def whole(*dims):
    return pl.BlockSpec(dims, lambda *_: (0,) * len(dims))


def per_head(*dims):
    return pl.BlockSpec((1,) + dims, lambda h, *_: (h,) + (0,) * len(dims))


def pick(dims, index):
    return pl.BlockSpec(dims, lambda h, *_: index(h))


def shape(dims, kind=BF16):
    return jax.ShapeDtypeStruct(dims, kind)


KV_ROWS = 8 * TOK + RANK
Q_ROWS = 4 * TOK + RANK
IN_ROWS = 512
HEAD_ROWS = 5 * RANK + 16


def pack_kernel(frozen_ref, normed_ref, down_ref, kv_ref, q_ref):
    out = lax.broadcasted_iota(jnp.int32, (256, 256), 0)
    source = lax.broadcasted_iota(jnp.int32, (256, 256), 1)
    order = (source == (out % 16) * 16 + ((out // 16) % 4) * 4 + out // 64).astype(BF16)
    for group in range(TOK // 16):
        rows = dot(order, frozen_ref[pl.ds(group * 256, 256), :]).astype(BF16)
        for zhi in range(4):
            for y in range(4):
                part = rows[(zhi * 4 + y) * 16 : (zhi * 4 + y) * 16 + 16]
                here = y * TOK + group * 16
                q_ref[zhi, pl.ds(here, 16), :] = part[:, :HD]
                kv_ref[zhi, pl.ds(here, 16), :] = part[:, HD : 2 * HD]
                kv_ref[zhi, pl.ds(4 * TOK + here, 16), :] = part[:, 2 * HD :]
    down_rows = dot(normed_ref[...], down_ref[...]).T.astype(BF16)
    for zhi in range(4):
        kv_ref[zhi, pl.ds(8 * TOK, RANK), :] = down_rows


def pack(frozen, normed, qkv_down):
    return call(
        pack_kernel,
        "pack",
        (1,),
        [whole(TOK * 16, 3 * HD), whole(TOK, 4096), whole(4096, RANK)],
        [whole(4, KV_ROWS, HD), whole(4, 4 * TOK, HD)],
        [shape((4, KV_ROWS, HD)), shape((4, 4 * TOK, HD))],
    )(frozen, normed, qkv_down)


def adapters_kernel(up_ref, ad_ref, rh_ref, out_up_ref, readout_ref, pack_ref):
    for part in range(3):
        pack_ref[pl.ds(part * RANK, RANK), :] = up_ref[:, part * HD : part * HD + HD]
    pack_ref[pl.ds(3 * RANK, RANK), :] = ad_ref[...].astype(F32).T.astype(BF16)
    pack_ref[pl.ds(4 * RANK, HD), :] = rh_ref[...]
    pack_ref[pl.ds(4 * RANK + HD, RANK), :] = dot(out_up_ref[...], readout_ref[...]).astype(BF16)


def adapters(up, ad, rh, out_up, readout):
    rows = 5 * RANK + HD
    return call(
        adapters_kernel,
        "adapters",
        (1,),
        [whole(RANK, 3 * HD), whole(HD, RANK), whole(HD, HD), whole(RANK, 256), whole(256, HD)],
        whole(rows, HD),
        shape((rows, HD)),
    )(up, ad, rh, out_up, readout)


def forward_kernel(*refs):
    keys, values, downs = refs[0:5], refs[5:10], refs[10:15]
    q_ref, fold_ref, wt_ref, cos_ref, sin_ref = refs[15:20]
    (att_ref, prob_ref, inv_ref, qo_ref, ko_ref, vo_ref, vel_ref, od_ref, folded_ref, dt_ref) = refs[20:30]
    rows_ref, vel_acc, od_acc = refs[30:]
    head = pl.program_id(0)

    def blocks(group):
        return [ref[i] for ref in group for i in range(ref.shape[0])]

    @pl.when(head == 0)
    def _():
        folded = fold_ref[0].astype(F32)
        for i in range(1, 4):
            folded = folded + fold_ref[i].astype(F32)
        folded_ref[...] = folded.astype(BF16)
        for i, block in enumerate(blocks(downs)):
            dt_ref[:, i * TOK : i * TOK + TOK] = block
            rows_ref[pl.ds(i * TOK, TOK), :] = block.astype(F32).T.astype(BF16)

    def rotated(tensor, cos, sin):
        return (tensor * cos + pltpu.roll(tensor, HD // 2, 1) * sin).astype(BF16)

    wt = wt_ref[0]
    down_rows = rows_ref[...]
    raw = jnp.concatenate([q_ref[i] for i in range(4)], axis=0).astype(F32)
    q = rotated(raw + dot(down_rows[:OWN], wt[:RANK]), cos_ref[:OWN, :], sin_ref[:OWN, :])
    raw = jnp.concatenate(blocks(keys), axis=0).astype(F32)
    k = rotated(raw + dot(down_rows, wt[RANK : 2 * RANK]), cos_ref[...], sin_ref[...])
    raw = jnp.concatenate(blocks(values), axis=0).astype(F32)
    v = (raw + dot(down_rows, wt[2 * RANK : 3 * RANK])).astype(BF16)
    qo_ref[0] = q
    ko_ref[0] = k
    vo_ref[0] = v
    scores = dot(k, q, (1, 1))
    peak = jnp.max(scores, axis=0, keepdims=True)
    weights = jnp.exp((scores - peak) * SCALE)
    inverse = 1.0 / jnp.sum(weights, axis=0, keepdims=True)
    weights = weights.astype(BF16)
    prob_ref[0] = weights
    inv_ref[0] = inverse
    attended = dot(v, weights, (0, 0)) * inverse
    att = attended.T.astype(BF16)
    att_ref[0] = att
    velocity = dot(att, wt[4 * RANK : 4 * RANK + HD])
    down = dot(att, wt[3 * RANK : 4 * RANK], (1, 1))

    @pl.when(head == 0)
    def _():
        vel_acc[...] = velocity
        od_acc[...] = down

    @pl.when(head > 0)
    def _():
        vel_acc[...] += velocity
        od_acc[...] += down

    @pl.when(head == HEADS - 1)
    def _():
        out_down = od_acc[...].astype(BF16)
        od_ref[...] = out_down
        vel_ref[...] = (vel_acc[...] + dot(out_down, folded_ref[...])).astype(BF16)


def forward(gathered, q, wts, cos, sin):
    def each(rows, index):
        return [pick((block.shape[0], rows, HD), index) for block in gathered]

    return call(
        forward_kernel,
        "attention_forward",
        (HEADS,),
        each(TOK, lambda h: (0, h, 0))
        + each(TOK, lambda h: (0, 4 + h, 0))
        + each(RANK, lambda h: (0, 8 * TOK // RANK, 0))
        + [
            pick((4, TOK, HD), lambda h: (0, h, 0)),
            pick((4, RANK, HD), lambda h: (0, 4 * TOK // RANK, 0)),
            per_head(5 * RANK + HD, HD),
            whole(LENGTH, HD),
            whole(LENGTH, HD),
        ],
        [
            per_head(OWN, HD),
            per_head(LENGTH, OWN),
            per_head(1, OWN),
            per_head(OWN, HD),
            per_head(LENGTH, HD),
            per_head(LENGTH, HD),
            whole(OWN, HD),
            whole(OWN, RANK),
            whole(RANK, HD),
            whole(RANK, LENGTH),
        ],
        [
            shape((HEADS, OWN, HD)),
            shape((HEADS, LENGTH, OWN)),
            shape((HEADS, 1, OWN), F32),
            shape((HEADS, OWN, HD)),
            shape((HEADS, LENGTH, HD)),
            shape((HEADS, LENGTH, HD)),
            shape((OWN, HD)),
            shape((OWN, RANK)),
            shape((RANK, HD)),
            shape((RANK, LENGTH)),
        ],
        [pltpu.VMEM((LENGTH, RANK), BF16), pltpu.VMEM((OWN, HD), F32), pltpu.VMEM((OWN, RANK), F32)],
    )(*gathered, *gathered, *gathered, q, q, wts, cos, sin)


def unrotate(grad, cos, sin):
    return (grad * cos - pltpu.roll(grad, HD // 2, 1) * sin).astype(BF16)


def backward_kernel(
    y_ref, mult_ref, vel_ref, res_ref, samp_ref, noise_ref, folded_ref, od_ref, q_ref, k_ref, v_ref, prob_ref,
    inv_ref, att_ref, wt_ref, dt_ref, cos_ref, sin_ref, dgrad_ref, small_ref, g_ref, og_ref, fg_ref, log_ref, dg_acc,
):
    head = pl.program_id(0)

    @pl.when(head == 0)
    def _():
        velocity = vel_ref[0].astype(F32)
        for i in range(1, 4):
            velocity = velocity + vel_ref[i].astype(F32)
        velocity = res_ref[0].astype(F32) + velocity
        gap = mult_ref[0, 0] * (velocity - samp_ref[0].astype(F32))
        noise = noise_ref[0].astype(F32)
        terms = jnp.sum(noise * gap + 0.5 * gap * gap, axis=0, keepdims=True)
        log = jnp.sum(terms, axis=1, keepdims=True) * (-1.0 / (LENGTH * HD))
        high = log.astype(BF16).astype(F32)
        middle = (log - high).astype(BF16).astype(F32)
        low = log - high - middle
        lane = lax.broadcasted_iota(jnp.int32, (16, HD), 1)
        rows = jnp.where(lane == 0, high, jnp.where(lane == 1, middle, jnp.where(lane == 2, low, 0.0)))
        log_ref[...] = rows.astype(BF16)
        g = (noise + gap).astype(BF16)
        g_ref[...] = g
        og_ref[...] = dot(g, folded_ref[...], (1, 1)).astype(BF16)
        fg_ref[...] = dot(od_ref[...], g, (0, 0)).astype(BF16)

    wt = wt_ref[0]
    att = att_ref[0]
    og = og_ref[...]
    att_grad = dot(g_ref[...], wt[4 * RANK : 4 * RANK + HD], (1, 1)) + dot(og, wt[3 * RANK : 4 * RANK])
    att_grad = att_grad.astype(BF16).astype(F32)
    inverse = inv_ref[0]
    delta = jnp.sum((att_grad * att.astype(F32)).T, axis=0, keepdims=True) * inverse
    scaled = (att_grad * jnp.broadcast_to(inverse, (HD, OWN)).T).astype(BF16)
    weights = prob_ref[0]
    prob_grad = dot(v_ref[0], scaled, (1, 1))
    score_grad = (weights.astype(F32) * (prob_grad - delta)).astype(BF16)
    v_grad = dot(weights, scaled).astype(BF16)
    k_grad = unrotate(dot(score_grad, q_ref[0]) * SCALE, cos_ref[...], sin_ref[...])
    q_grad = dot(k_ref[0], score_grad, (0, 0)) * SCALE
    q_grad = unrotate(q_grad.T, cos_ref[:OWN, :], sin_ref[:OWN, :])
    share = dot(wt[RANK : 2 * RANK], k_grad, (1, 1)) + dot(wt[2 * RANK : 3 * RANK], v_grad, (1, 1))
    mine = share[:, :OWN] + dot(wt[:RANK], q_grad, (1, 1))

    @pl.when(head == 0)
    def _():
        dg_acc[:, :OWN] = mine
        dg_acc[:, OWN:] = share[:, OWN:]

    @pl.when(head > 0)
    def _():
        dg_acc[:, :OWN] += mine
        dg_acc[:, OWN:] += share[:, OWN:]

    down_t = dt_ref[...]
    small_ref[0, :RANK, :] = dot(down_t[:, :OWN], q_grad).astype(BF16)
    small_ref[0, RANK : 2 * RANK, :] = dot(down_t, k_grad).astype(BF16)
    small_ref[0, 2 * RANK : 3 * RANK, :] = dot(down_t, v_grad).astype(BF16)
    small_ref[0, 3 * RANK : 4 * RANK, :] = dot(og, att, (0, 0)).astype(BF16)
    small_ref[0, 4 * RANK : 5 * RANK, :] = fg_ref[...]
    small_ref[0, 5 * RANK :, :] = log_ref[...]

    @pl.when(head == HEADS - 1)
    def _():
        for near in range(4):
            for zhi in range(4):
                place = ((y_ref[0] + near) % 4) * 4 + zhi
                first = (near * 4 + zhi) * TOK
                dgrad_ref[pl.ds(place, 1)] = dg_acc[:, first : first + TOK].astype(BF16)[None]


def backward(y, mult, velocity, residual, sampling, noise, folded, out_down, q, k, v, prob, inv, att, wts, down_t, cos, sin):
    mine = pl.BlockSpec((1, OWN, HD), lambda h, y_ref: (0, y_ref[0], 0))
    return call(
        backward_kernel,
        "attention_backward",
        (HEADS,),
        [
            pl.BlockSpec(memory_space=pltpu.SMEM),
            whole(4, OWN, HD),
            mine,
            mine,
            mine,
            whole(RANK, HD),
            whole(OWN, RANK),
            per_head(OWN, HD),
            per_head(LENGTH, HD),
            per_head(LENGTH, HD),
            per_head(LENGTH, OWN),
            per_head(1, OWN),
            per_head(OWN, HD),
            per_head(5 * RANK + HD, HD),
            whole(RANK, LENGTH),
            whole(LENGTH, HD),
            whole(LENGTH, HD),
        ],
        [whole(16, RANK, TOK), per_head(HEAD_ROWS, HD)],
        [shape((16, RANK, TOK)), shape((HEADS, HEAD_ROWS, HD))],
        [
            pltpu.VMEM((OWN, HD), BF16),
            pltpu.VMEM((OWN, RANK), BF16),
            pltpu.VMEM((RANK, HD), BF16),
            pltpu.VMEM((16, HD), BF16),
            pltpu.VMEM((RANK, LENGTH), F32),
        ],
        prefetch=1,
    )(y, mult, velocity, residual, sampling, noise, folded, out_down, q, k, v, prob, inv, att, wts, down_t, cos, sin)


def grad_in_kernel(shares_ref, normed_ref, small_ref, out_ref):
    down_grad = shares_ref[0].astype(F32)
    for i in range(1, 16):
        down_grad = down_grad + shares_ref[i].astype(F32)
    grad = dot(down_grad.astype(BF16), normed_ref[...])
    for j in range(16):
        left = grad[:, j * TOK : j * TOK + TOK]
        right = grad[:, 2048 + j * TOK : 2048 + j * TOK + TOK]
        block = jnp.concatenate([left, right], axis=0).T.astype(BF16)
        for y in range(4):
            out_ref[y, pl.ds(j * 32, 32), :] = block[y * 32 : y * 32 + 32]
    for y in range(4):
        out_ref[y, pl.ds(IN_ROWS, HEAD_ROWS), :] = small_ref[y]


def grad_in_part(shares, normed, small):
    rows = IN_ROWS + HEAD_ROWS
    return call(
        grad_in_kernel,
        "grad_in_part",
        (1,),
        [whole(16, RANK, TOK), whole(TOK, 4096), whole(4, HEAD_ROWS, HD)],
        whole(4, rows, HD),
        shape((4, rows, HD)),
    )(shares, normed, small)


def weigh_kernel(scal_ref, got_ref, out_ref):
    total = got_ref[0].astype(F32)
    for i in range(1, 4):
        total = total + got_ref[i].astype(F32)
    lane = lax.broadcasted_iota(jnp.int32, (8, HD), 1)
    log = total[IN_ROWS + 5 * RANK : IN_ROWS + 5 * RANK + 8]
    log = jnp.sum(jnp.where(lane < 3, log, 0.0), axis=1, keepdims=True)
    ratio = jnp.exp(log[:1])
    advantage = scal_ref[0, 0]
    positive = jnp.where(advantage >= 0.0, 1.0, 0.0)
    active = jnp.where(ratio <= 1.0 + CLIP, positive, 0.0) + jnp.where(ratio >= 1.0 - CLIP, 1.0 - positive, 0.0)
    weight = jnp.where(active > 0.5, -advantage * scal_ref[0, 1] * ratio, 0.0)
    total = total[: IN_ROWS + 5 * RANK] * weight
    for xc in range(8):
        for low in range(2):
            out_ref[xc, pl.ds(low * 32, 32), :] = total[(low * 8 + xc) * 32 : (low * 8 + xc) * 32 + 32].astype(BF16)
    out = lax.broadcasted_iota(jnp.int32, (RANK, RANK), 0)
    source = lax.broadcasted_iota(jnp.int32, (RANK, RANK), 1)
    order = (source == ((out // 2) % 4) * 16 + (out // 8) * 2 + out % 2).astype(BF16)
    parts = []
    for i in range(5):
        rows = total[IN_ROWS + i * RANK : IN_ROWS + i * RANK + RANK].astype(BF16)
        parts.append(dot(order, rows))
    for xc in range(8):
        rows = [part[xc * 8 : xc * 8 + 8] for part in parts] + [jnp.zeros((8, HD), F32)]
        out_ref[xc, pl.ds(64, 48), :] = jnp.concatenate(rows, axis=0).astype(BF16)


def weigh(scalars, got):
    return call(
        weigh_kernel,
        "weigh",
        (1,),
        [pl.BlockSpec(memory_space=pltpu.SMEM), whole(4, IN_ROWS + HEAD_ROWS, HD)],
        whole(8, 112, HD),
        shape((8, 112, HD)),
    )(scalars, got)


def body(
    normed,
    frozen,
    frames,
    qkv_down,
    qkv_up,
    out_down_adapter,
    out_up,
    readout,
    readout_head,
    residual_velocity,
    sampling_velocity,
    sampler_step_noise,
    rewards,
    rollout_group_index,
    denoising_step_index,
):
    y = lax.axis_index("y")
    zhi = lax.axis_index("zhi")
    ahead = [(i, (i + 1) % 4) for i in range(4)]
    back = [(i, (i + 3) % 4) for i in range(4)]

    send_kv, send_q = pack(frozen.reshape(TOK * 16, 3 * HD), normed[0], qkv_down)
    mine = exchange(send_kv, "zhi")
    before = lax.ppermute(mine, "y", ahead)
    after = lax.ppermute(mine, "y", back)
    far_low = lax.ppermute(after[:2], "y", back)
    far_high = lax.ppermute(before[2:], "y", ahead)

    wts = adapters(qkv_up[:, 0], out_down_adapter[0], readout_head[0], out_up, readout)
    wts = lax.all_gather(wts, "y", axis=0, tiled=False)
    fold_y = jnp.sum(wts[:, 4 * RANK + HD :].astype(F32), axis=0).astype(BF16)
    fold_y = jnp.broadcast_to(fold_y[None], (4, RANK, HD))
    q_raw = exchange(jnp.concatenate([send_q, fold_y], axis=1), "zhi")

    multiplier = gap_factor(denoising_step_index)
    advantage = advantages(rewards, rollout_group_index)[lax.axis_index(DP)]
    scalars = jnp.stack([advantage, multiplier])[None]
    cos, sin = rope_tables(jnp.roll(frames[0], -y * OWN))

    att, prob, inv, q, k, v, vel_part, out_down, folded, down_t = forward(
        (mine, after, far_low, far_high, before), q_raw, wts, cos, sin
    )
    velocity = lax.all_gather(vel_part, "zhi", axis=0, tiled=False)
    down_grad, small = backward(
        y[None].astype(jnp.int32), multiplier[None, None], velocity, residual_velocity, sampling_velocity,
        sampler_step_noise, folded, out_down, q, k, v, prob, inv, att, wts, down_t, cos, sin,
    )

    down_grad = exchange(down_grad, SEQ)
    both = weigh(scalars, exchange(grad_in_part(down_grad, normed[0], small), "y"))
    both = jnp.sum(exchange(both, XC).astype(F32), axis=0)
    in_part = both[:64].reshape(2, 4, 8, 2, 64).transpose(3, 0, 1, 2, 4).reshape(4, 4, 4, HD)
    small = both[64:104].reshape(5, 4, 2, HD).transpose(1, 2, 0, 3).reshape(4, 1, 10, HD)
    here = (lax.broadcasted_iota(jnp.int32, (4, 4, 10, HD), 1) == zhi).astype(F32)
    everywhere = lax.broadcasted_iota(jnp.int32, (4, 4, 10, HD), 2) % 5 == 4
    small = small * jnp.where(everywhere, 1.0, here)
    last = jnp.concatenate([in_part, small, jnp.zeros((4, 4, 2, HD), F32)], axis=2).astype(BF16)
    last = jnp.sum(exchange(last.reshape(16, 16, HD), Z).astype(F32), axis=0)
    grad_in = last[:4].reshape(8, 64)
    small = last[4:14].reshape(2, 5, HD)
    grad_qkv = small[:, None, :3].reshape(2, 1, 3 * HD)
    grad_out_in = small[:, 3].T[None]
    grad_out = lax.dot_general(
        small[:, 4], readout.astype(F32), (((1,), (1,)), ((), ())), precision=lax.Precision.HIGHEST
    )
    return grad_in, grad_qkv, grad_out_in, grad_out


def solution(mesh):
    mesh = Mesh(mesh.devices.reshape(SIZES), NAMES)
    in_specs = (
        P(DP, SEQ, None),
        P(DP, SEQ, None, None),
        P(DP, None),
        P(),
        P(None, SEQ, None),
        P(SEQ, None, None),
        P(None, SEQ),
        P(SEQ, None),
        P(SEQ, None, None),
        P(DP, None, None),
        P(DP, None, None),
        P(DP, None, None),
        P(),
        P(),
        P(),
    )
    out_specs = (P(DP + SEQ, None), P(DP, SEQ, None), P(SEQ, None, DP), P(DP, SEQ))
    return jax.shard_map(body, mesh=mesh, in_specs=in_specs, out_specs=out_specs, check_vma=False)
```
